32 devices in a mesh: box: 2 (over x), slab: 8 (over z, y), chan: 2 (over core).
Axes of the slice: x: 2, y: 2, z: 4, core: 2. Of those that a mesh axis runs over, the one named last changes fastest.
Arguments:
- field: bfloat16 [64, 128, 4096], P(('box', 'slab'), 'chan'), parts along dimension 0, may hold values from -6 to 6
- conv_one: bfloat16 [3, 3, 3, 128, 128], P(None, None, None, 'chan'), may hold values from -0.109375 to 0.109375
- bias_one: float32 [128], P('chan'), may hold values from -3 to 3
- conv_two: bfloat16 [3, 3, 3, 128, 128], replicated, may hold values from -0.109375 to 0.109375
- bias_two: float32 [128], P('chan'), may hold values from -3 to 3
Outputs:
- block_out: bfloat16 [64, 128, 4096], P(('box', 'slab'), 'chan'), parts along dimension 0
The draws below stay inside these ranges and needn't reach their ends.
There are 2 independent parts, one for each index of `box`. The reference program is written for one: setup_inputs(seed, part) draws one part's arguments, and reference() takes and returns one part's arrays. A program takes and returns all parts, laid end to end along the dimension named above; an argument that names none is the same for every part. Nothing has to cross between parts.
All inputs are finite; a program needn't handle non-finite values.
Results may differ from the reference program's by a relative error of at most 0.0034.
Values may be sent and summed in bfloat16 or wider, within the bound.
A program may use at most 64 MiB of HBM per device.

```python
import jax
import jax.numpy as jnp
from jax import lax

C = 128
SIDE = 64
NZ = 32


def level_of(own_key, dims, cuts, low, top_value):
    loudness = 1.0
    for position, parts in cuts:
        draws = jax.random.uniform(jax.random.fold_in(jax.random.fold_in(own_key, 6), position), (parts,), jnp.float32, low / len(cuts), top_value / len(cuts))
        loudness = loudness * jnp.repeat(jnp.exp(draws), dims[position] // parts).reshape((-1,) + (1,) * (len(dims) - 1 - position))
    return loudness


def normal_values(own_key, extent, deviation, bound, pieces=(), dtype=jnp.bfloat16):
    entries = deviation * jax.random.normal(own_key, extent, jnp.float32)
    if pieces:
        entries = entries * level_of(own_key, extent, pieces, -0.22, 0.18)
    return jnp.clip(entries, -bound, bound).astype(dtype)


def setup_inputs(seed: int = 0, part: int = 0) -> dict:
    seeds = jax.random.split(jax.random.key(seed), 6)
    part_splits = jax.random.split(jax.random.fold_in(seeds[5], part), 6)
    field = normal_values(part_splits[0], (NZ, C, SIDE * SIDE), 1.0, 6.0, ((0, 8), (1, 2)))
    conv_one = normal_values(seeds[1], (3, 3, 3, C, C), (27 * C) ** -0.5, 0.109375, ((3, 2),))
    bias_one = normal_values(seeds[2], (C,), 0.5, 3.0, ((0, 2),), jnp.float32)
    conv_two = normal_values(seeds[3], (3, 3, 3, C, C), (27 * C) ** -0.5, 0.109375)
    bias_two = normal_values(seeds[4], (C,), 0.5, 3.0, ((0, 2),), jnp.float32)
    return dict(field=field, conv_one=conv_one, bias_one=bias_one, conv_two=conv_two, bias_two=bias_two)


def convolve(values, kernel):
    planes, width, cells = values.shape
    grid = values.reshape(planes, width, SIDE, SIDE)
    padded = jnp.pad(grid, ((1, 1), (0, 0), (1, 1), (1, 1)), mode="wrap")
    result = lax.conv_general_dilated(padded[None], kernel, (1, 1, 1), "VALID", dimension_numbers=("NDCHW", "DHWOI", "NDCHW"), preferred_element_type=jnp.float32)
    return result[0].reshape(planes, kernel.shape[3], cells)


def reference(field, conv_one, bias_one, conv_two, bias_two):
    hidden = jnp.maximum(convolve(field, conv_one) + bias_one[:, None], 0.0).astype(jnp.bfloat16)
    total = convolve(hidden, conv_two) + bias_two[:, None] + field.astype(jnp.float32)
    return jnp.maximum(total, 0.0).astype(jnp.bfloat16)
```

```python
import functools

import jax
import jax.numpy as jnp
from jax import lax
from jax.experimental import pallas as pl
from jax.experimental.pallas import tpu as pltpu
from jax.sharding import PartitionSpec as P

SIDE = 64
CELLS = SIDE * SIDE
CHUNKS = 8
ROWS = SIDE // CHUNKS
SPAN = ROWS * SIDE
WIDTH = 128
HALF = WIDTH // 2
MESH = pl.DeviceIdType.MESH


def kernel(
    slabs,
    field, conv_one, conv_two, bias,
    out,
    raw, taps_one, taps_two, raw_one, raw_two, field_wide, hidden_wide, result, biases,
    weight_sem, near_send, near_recv, near_local, far_send, far_recv,
    hidden_send, hidden_recv, out_send, out_recv, out_local,
):
    rank = lax.axis_index("chan")
    slab = lax.axis_index("slab")
    other = 1 - rank
    after = lax.rem(slab + 1, slabs)
    before = lax.rem(slab + slabs - 1, slabs)
    beyond = lax.rem(slab + 2 * rank + slabs - 1, slabs)
    sibling = {"chan": other, "slab": slab}

    barrier = pltpu.get_barrier_semaphore()
    for target in (sibling, {"chan": 0, "slab": beyond}, {"chan": 1, "slab": beyond}):
        pl.semaphore_signal(barrier, inc=1, device_id=target, device_id_type=MESH)

    own = pl.ds(pl.multiple_of(rank * HALF, HALF), HALF)
    theirs = pl.ds(pl.multiple_of(other * HALF, HALF), HALF)

    def part(j):
        return pl.ds(pl.multiple_of(j * SPAN, SPAN), SPAN)

    def remote(src, dst, send, recv, target):
        return pltpu.make_async_remote_copy(
            src_ref=src, dst_ref=dst, send_sem=send, recv_sem=recv,
            device_id=target, device_id_type=MESH,
        )

    def far(j, up):
        plane = 3 if up else 0
        return remote(
            field.at[plane, :, part(j)],
            raw.at[0 if up else 3, own, part(j)],
            far_send.at[0 if up else 1, j],
            far_recv.at[rank, j],
            {"chan": 0, "slab": after} if up else {"chan": 1, "slab": before},
        )

    def near(i):
        return remote(
            field.at[other + i], raw.at[rank + i, own], near_send.at[i], near_recv.at[i], sibling
        )

    def near_own(i):
        return pltpu.make_async_copy(
            field.at[rank + i], raw.at[other + i, own], near_local.at[i]
        )

    send_taps = remote(
        conv_one, raw_one.at[:, own], weight_sem.at[0], weight_sem.at[1], sibling
    )
    send_bias = remote(bias, biases.at[1], weight_sem.at[2], weight_sem.at[3], sibling)
    own_taps = pltpu.make_async_copy(conv_one, raw_one.at[:, own], weight_sem.at[4])
    own_bias = pltpu.make_async_copy(bias, biases.at[0], weight_sem.at[5])
    own_two = pltpu.make_async_copy(conv_two, raw_two, weight_sem.at[6])

    own_taps.start()
    for i in range(3):
        near_own(i).start()
    own_bias.start()
    own_two.start()
    pl.semaphore_wait(barrier, 3)

    send_taps.start()
    send_bias.start()

    def start_far(i):
        j = lax.rem(i + CHUNKS - 1, CHUNKS)
        far(j, True).start()
        far(j, False).start()

    pl.loop(0, CHUNKS)(start_far)
    for i in range(3):
        near(i).start()

    def spread(wide, plane, j, values, centre):
        cells = values.reshape(ROWS, SIDE, WIDTH)
        turned = (pltpu.roll(cells, 1, 1), cells, pltpu.roll(cells, SIDE - 1, 1))
        for c in range(3):
            flat = turned[c].reshape(SPAN, WIDTH).astype(jnp.bfloat16)
            if c != 1 or centre:
                start = pl.multiple_of((j * ROWS + 1) * SIDE, SIDE)
                wide[plane, c, pl.ds(start, SPAN), :] = flat

            @pl.when(j == 0)
            def _():
                wide[plane, c, (SIDE + 1) * SIDE:(SIDE + 2) * SIDE, :] = flat[:SIDE]

            @pl.when(j == CHUNKS - 1)
            def _():
                wide[plane, c, 0:SIDE, :] = flat[SPAN - SIDE:]

    def build(taps, source):
        taps[0:9 * WIDTH, WIDTH:] = jnp.zeros((9 * WIDTH, WIDTH), jnp.bfloat16)
        taps[27 * WIDTH:, :WIDTH] = jnp.zeros((9 * WIDTH, WIDTH), jnp.bfloat16)

        @pl.loop(0, 27)
        def _(t):
            block = source[t].T
            here = pl.multiple_of(t * WIDTH, WIDTH)
            taps[pl.ds(here, WIDTH), :WIDTH] = block
            later = pl.multiple_of((t + 9) * WIDTH, WIDTH)
            taps[pl.ds(later, WIDTH), WIDTH:] = block

    def product(wide, taps, j):
        pieces = []
        for plane in range(4):
            for b in range(3):
                start = pl.multiple_of((j * ROWS + b) * SIDE, SIDE)
                for c in range(3):
                    pieces.append(wide[plane, c, pl.ds(start, SPAN), :])
        return jnp.dot(
            jnp.concatenate(pieces, axis=1), taps[...], preferred_element_type=jnp.float32
        )

    def turn(plane, j):
        values = raw[plane, :, part(j)].astype(jnp.float32).T
        spread(field_wide, plane, j, values, True)

    own_taps.wait()
    send_taps.wait()
    build(taps_one, raw_one)
    own_bias.wait()
    send_bias.wait()

    for i in range(3):
        near_own(i).wait()
        near(i).wait_send()
        pltpu.make_async_remote_copy(
            src_ref=field.at[rank + i], dst_ref=raw.at[other + i, theirs],
            send_sem=near_send.at[i], recv_sem=near_recv.at[i],
            device_id=sibling, device_id_type=MESH,
        ).wait_recv()
        pl.loop(0, CHUNKS)(functools.partial(turn, other + i))

    edge = 3 * rank

    def arrive(j):
        for half in range(2):
            pltpu.make_async_remote_copy(
                src_ref=field.at[0, :, part(j)],
                dst_ref=raw.at[edge, half * HALF:(half + 1) * HALF, part(j)],
                send_sem=far_send.at[half, j], recv_sem=far_recv.at[half, j],
                device_id=sibling, device_id_type=MESH,
            ).wait_recv()
        turn(edge, j)

    down_to = {"chan": other, "slab": lax.rem(slab + rank + slabs - 1, slabs)}
    up_to = {"chan": other, "slab": lax.rem(slab + rank, slabs)}

    def here(j):
        return pl.ds(pl.multiple_of((j * ROWS + 1) * SIDE, SIDE), SPAN)

    def hand(j, up):
        return remote(
            hidden_wide.at[2 if up else 1, 1, here(j)],
            hidden_wide.at[0 if up else 3, 1, here(j)],
            hidden_send.at[0 if up else 1, j],
            hidden_recv.at[0 if up else 1, j],
            up_to if up else down_to,
        )

    def first(j):
        offsets = biases[0, 0:1, :] + biases[1, 0:1, :]
        total = product(field_wide, taps_one, j)
        for z in range(2):
            values = jnp.maximum(total[:, z * WIDTH:(z + 1) * WIDTH] + offsets, 0.0)
            values = values.astype(jnp.bfloat16).astype(jnp.float32)
            spread(hidden_wide, 1 + z, j, values, True)
        hand(j, False).start()
        hand(j, True).start()

    arrive(CHUNKS - 1)
    arrive(0)

    @pl.loop(0, CHUNKS)
    def _(j):
        @pl.when(j < CHUNKS - 2)
        def _():
            arrive(j + 1)

        first(j)

    own_two.wait()
    build(taps_two, raw_two)

    def receive(j):
        for up in (True, False):
            hand(j, up).wait_recv()
            plane = 0 if up else 3
            values = hidden_wide[plane, 1, here(j), :].astype(jnp.float32)
            spread(hidden_wide, plane, j, values, False)

    def give(j):
        return remote(
            result.at[:, theirs, part(j)], out.at[pl.ds(2 * rank, 2), :, part(j)],
            out_send.at[j], out_recv.at[j], sibling,
        )

    def keep(j):
        return pltpu.make_async_copy(
            result.at[:, own, part(j)], out.at[pl.ds(2 * rank, 2), :, part(j)], out_local.at[j]
        )

    def second(j):
        offsets = biases[0, 1:2, :] + biases[1, 1:2, :]
        total = product(hidden_wide, taps_two, j)
        for z in range(2):
            values = total[:, z * WIDTH:(z + 1) * WIDTH] + offsets
            values = values + field_wide[1 + z, 1, here(j), :].astype(jnp.float32)
            values = jnp.maximum(values, 0.0)
            result[z, :, part(j)] = values.T.astype(jnp.bfloat16)
        give(j).start()
        keep(j).start()

    receive(0)
    receive(1)

    @pl.loop(1, CHUNKS + 1)
    def _(j):
        @pl.when(j < CHUNKS - 1)
        def _():
            receive(j + 1)

        second(lax.rem(j, CHUNKS))

    @pl.loop(0, CHUNKS)
    def _(j):
        far(j, True).wait_send()
        far(j, False).wait_send()
        hand(j, True).wait_send()
        hand(j, False).wait_send()
        keep(j).wait()
        give(j).wait_send()
        pltpu.make_async_remote_copy(
            src_ref=result.at[:, theirs, part(j)],
            dst_ref=out.at[pl.ds(2 * other, 2), :, part(j)],
            send_sem=out_send.at[j], recv_sem=out_recv.at[j],
            device_id=sibling, device_id_type=MESH,
        ).wait_recv()


def body(field, conv_one, bias_one, conv_two, bias_two):
    rank = lax.axis_index("chan")
    pair = jnp.stack([bias_one, bias_two])
    own = (jnp.arange(2) == rank)[None, :, None]
    bias = jnp.where(own, pair[:, None, :], 0.0).reshape(2, WIDTH)
    bias = jnp.pad(bias, ((0, 6), (0, 0)))
    anywhere = pl.BlockSpec(memory_space=pl.ANY)
    bf16 = jnp.bfloat16
    padded = (SIDE + 2) * SIDE
    dma = pltpu.SemaphoreType.DMA
    return pl.pallas_call(
        functools.partial(kernel, lax.axis_size("slab")),
        out_shape=jax.ShapeDtypeStruct(field.shape, field.dtype),
        in_specs=[anywhere] * 4,
        out_specs=anywhere,
        scratch_shapes=[
            pltpu.VMEM((4, WIDTH, CELLS), bf16),
            pltpu.VMEM((36 * WIDTH, 2 * WIDTH), bf16),
            pltpu.VMEM((36 * WIDTH, 2 * WIDTH), bf16),
            pltpu.VMEM((27, WIDTH, WIDTH), bf16),
            pltpu.VMEM((27, WIDTH, WIDTH), bf16),
            pltpu.VMEM((4, 3, padded, WIDTH), bf16),
            pltpu.VMEM((4, 3, padded, WIDTH), bf16),
            pltpu.VMEM((2, WIDTH, CELLS), bf16),
            pltpu.VMEM((2, 8, WIDTH), jnp.float32),
            dma((7,)),
            dma((3,)), dma((3,)), dma((3,)),
            dma((2, CHUNKS)), dma((2, CHUNKS)),
            dma((2, CHUNKS)), dma((2, CHUNKS)),
            dma((CHUNKS,)), dma((CHUNKS,)), dma((CHUNKS,)),
        ],
        compiler_params=pltpu.CompilerParams(
            collective_id=0, has_side_effects=True, vmem_limit_bytes=56 * 2**20
        ),
        cost_estimate=pl.CostEstimate(
            flops=2 * 2 * 2 * CELLS * WIDTH * 27 * WIDTH, bytes_accessed=8 * 2**20,
            transcendentals=0,
        ),
    )(field, conv_one.reshape(27, HALF, WIDTH), conv_two.reshape(27, WIDTH, WIDTH), bias)


def solution(mesh):
    return jax.shard_map(
        body,
        mesh=mesh,
        in_specs=(
            P(("box", "slab"), "chan", None),
            P(None, None, None, "chan", None),
            P("chan"),
            P(),
            P("chan"),
        ),
        out_specs=P(("box", "slab"), "chan", None),
        check_vma=False,
    )
```

```python
import functools

import jax
import jax.numpy as jnp
from jax import lax
from jax.experimental import pallas as pl
from jax.experimental.pallas import tpu as pltpu
from jax.sharding import PartitionSpec as P

SIDE = 64
DEPTH = 4
CELLS = SIDE * SIDE
CHUNKS = 8
ROWS = SIDE // CHUNKS
SPAN = ROWS * SIDE
WIDTH = 128
HALF = WIDTH // 2
MESH = pl.DeviceIdType.MESH


def kernel(
    slabs,
    field, conv_one, conv_two, bias,
    out,
    raw, taps_one, taps_two, raw_one, raw_two, field_wide, hidden_wide, result, biases,
    weight_sem, near_send, near_recv, near_local, far_send, far_recv,
    hidden_send, hidden_recv, out_send, out_recv, out_local,
):
    rank = lax.axis_index("chan")
    slab = lax.axis_index("slab")
    other = 1 - rank
    after = lax.rem(slab + 1, slabs)
    before = lax.rem(slab + slabs - 1, slabs)
    beyond = lax.rem(slab + 2 * rank + slabs - 1, slabs)
    sibling = {"chan": other, "slab": slab}

    barrier = pltpu.get_barrier_semaphore()
    for target in (sibling, {"chan": 0, "slab": beyond}, {"chan": 1, "slab": beyond}):
        pl.semaphore_signal(barrier, inc=1, device_id=target, device_id_type=MESH)

    own = pl.ds(pl.multiple_of(rank * HALF, HALF), HALF)
    theirs = pl.ds(pl.multiple_of(other * HALF, HALF), HALF)

    def part(j):
        return pl.ds(pl.multiple_of(j * SPAN, SPAN), SPAN)

    def remote(src, dst, send, recv, target):
        return pltpu.make_async_remote_copy(
            src_ref=src, dst_ref=dst, send_sem=send, recv_sem=recv,
            device_id=target, device_id_type=MESH,
        )

    def far(j, up):
        plane = 3 if up else 0
        return remote(
            field.at[plane, :, part(j)],
            raw.at[0 if up else 3, own, part(j)],
            far_send.at[0 if up else 1, j],
            far_recv.at[rank, j],
            {"chan": 0, "slab": after} if up else {"chan": 1, "slab": before},
        )

    def near(i):
        return remote(
            field.at[other + i], raw.at[rank + i, own], near_send.at[i], near_recv.at[i], sibling
        )

    def near_own(i):
        return pltpu.make_async_copy(
            field.at[rank + i], raw.at[other + i, own], near_local.at[i]
        )

    send_taps = remote(
        conv_one, raw_one.at[:, own], weight_sem.at[0], weight_sem.at[1], sibling
    )
    send_bias = remote(bias, biases.at[1], weight_sem.at[2], weight_sem.at[3], sibling)
    own_taps = pltpu.make_async_copy(conv_one, raw_one.at[:, own], weight_sem.at[4])
    own_bias = pltpu.make_async_copy(bias, biases.at[0], weight_sem.at[5])
    own_two = pltpu.make_async_copy(conv_two, raw_two, weight_sem.at[6])

    own_taps.start()
    for i in range(3):
        near_own(i).start()
    own_bias.start()
    own_two.start()
    pl.semaphore_wait(barrier, 3)

    send_taps.start()
    send_bias.start()

    def start_far(i):
        j = lax.rem(i + CHUNKS - 1, CHUNKS)
        far(j, True).start()
        far(j, False).start()

    def end_far(i):
        j = lax.rem(i + CHUNKS - 1, CHUNKS)
        far(j, True).wait_send()
        far(j, False).wait_send()

    start_far(0)
    for i in range(3):
        near(i).start()
    for i in range(1, DEPTH):
        start_far(i)

    def spread(wide, plane, j, values, centre):
        cells = values.reshape(ROWS, SIDE, WIDTH)
        turned = (pltpu.roll(cells, 1, 1), cells, pltpu.roll(cells, SIDE - 1, 1))
        for c in range(3):
            flat = turned[c].reshape(SPAN, WIDTH).astype(jnp.bfloat16)
            if c != 1 or centre:
                start = pl.multiple_of((j * ROWS + 1) * SIDE, SIDE)
                wide[plane, c, pl.ds(start, SPAN), :] = flat

            @pl.when(j == 0)
            def _():
                wide[plane, c, (SIDE + 1) * SIDE:(SIDE + 2) * SIDE, :] = flat[:SIDE]

            @pl.when(j == CHUNKS - 1)
            def _():
                wide[plane, c, 0:SIDE, :] = flat[SPAN - SIDE:]

    def build(taps, source):
        taps[0:9 * WIDTH, WIDTH:] = jnp.zeros((9 * WIDTH, WIDTH), jnp.bfloat16)
        taps[27 * WIDTH:, :WIDTH] = jnp.zeros((9 * WIDTH, WIDTH), jnp.bfloat16)

        @pl.loop(0, 27)
        def _(t):
            block = source[t].T
            here = pl.multiple_of(t * WIDTH, WIDTH)
            taps[pl.ds(here, WIDTH), :WIDTH] = block
            later = pl.multiple_of((t + 9) * WIDTH, WIDTH)
            taps[pl.ds(later, WIDTH), WIDTH:] = block

    def product(wide, taps, j):
        pieces = []
        for plane in range(4):
            for b in range(3):
                start = pl.multiple_of((j * ROWS + b) * SIDE, SIDE)
                for c in range(3):
                    pieces.append(wide[plane, c, pl.ds(start, SPAN), :])
        return jnp.dot(
            jnp.concatenate(pieces, axis=1), taps[...], preferred_element_type=jnp.float32
        )

    def turn(plane, j):
        values = raw[plane, :, part(j)].astype(jnp.float32).T
        spread(field_wide, plane, j, values, True)

    own_taps.wait()
    send_taps.wait()
    build(taps_one, raw_one)
    own_bias.wait()
    send_bias.wait()

    for i in range(3):
        near_own(i).wait()
        near(i).wait_send()
        pltpu.make_async_remote_copy(
            src_ref=field.at[rank + i], dst_ref=raw.at[other + i, theirs],
            send_sem=near_send.at[i], recv_sem=near_recv.at[i],
            device_id=sibling, device_id_type=MESH,
        ).wait_recv()
        pl.loop(0, CHUNKS)(functools.partial(turn, other + i))

    edge = 3 * rank

    def arrive(j):
        for half in range(2):
            pltpu.make_async_remote_copy(
                src_ref=field.at[0, :, part(j)],
                dst_ref=raw.at[edge, half * HALF:(half + 1) * HALF, part(j)],
                send_sem=far_send.at[half, j], recv_sem=far_recv.at[half, j],
                device_id=sibling, device_id_type=MESH,
            ).wait_recv()
        turn(edge, j)

    down_to = {"chan": other, "slab": lax.rem(slab + rank + slabs - 1, slabs)}
    up_to = {"chan": other, "slab": lax.rem(slab + rank, slabs)}

    def here(j):
        return pl.ds(pl.multiple_of((j * ROWS + 1) * SIDE, SIDE), SPAN)

    def lines(m):
        return pl.ds(pl.multiple_of((m * ROWS + 2) * SIDE, SIDE), SPAN)

    head = pl.ds(ROWS * SIDE, 2 * SIDE)
    tail = pl.ds(2 * SIDE, (ROWS - 2) * SIDE)

    def hand(m, up, cells):
        return remote(
            hidden_wide.at[2 if up else 1, 1, cells],
            hidden_wide.at[0 if up else 3, 1, cells],
            hidden_send.at[0 if up else 1, m],
            hidden_recv.at[0 if up else 1, m],
            up_to if up else down_to,
        )

    def hand_both(m, cells):
        hand(m, False, cells).start()
        hand(m, True, cells).start()

    def first(j):
        offsets = biases[0, 0:1, :] + biases[1, 0:1, :]
        total = product(field_wide, taps_one, j)
        for z in range(2):
            values = jnp.maximum(total[:, z * WIDTH:(z + 1) * WIDTH] + offsets, 0.0)
            values = values.astype(jnp.bfloat16).astype(jnp.float32)
            spread(hidden_wide, 1 + z, j, values, True)
    end_far(0)
    start_far(DEPTH)
    arrive(CHUNKS - 1)
    end_far(1)
    start_far(DEPTH + 1)
    arrive(0)

    @pl.loop(0, CHUNKS)
    def _(j):
        @pl.when(j < CHUNKS - 2)
        def _():
            arrive(j + 1)
            end_far(j + 2)

            @pl.when(j + 2 + DEPTH < CHUNKS)
            def _():
                start_far(j + 2 + DEPTH)

        @pl.when(j == CHUNKS - 4)
        def _():
            hand_both(CHUNKS, head)
            hand_both(1, lines(1))

        @pl.when(j == CHUNKS - 3)
        def _():
            pl.loop(2, CHUNKS - 4)(lambda m: hand_both(m, lines(m)))

        first(j)

        @pl.when(j >= CHUNKS - 3)
        def _():
            hand_both(j - 1, lines(j - 1))

    hand_both(CHUNKS - 1, lines(CHUNKS - 1))
    hand_both(0, tail)

    own_two.wait()
    build(taps_two, raw_two)

    def receive(m, cells, rows):
        for up in (True, False):
            hand(m, up, cells).wait_recv()
            plane = 0 if up else 3
            values = hidden_wide[plane, 1, cells, :].astype(jnp.float32)
            grid = values.reshape(rows, SIDE, WIDTH)
            turned = (pltpu.roll(grid, 1, 1), grid, pltpu.roll(grid, SIDE - 1, 1))
            for c in range(3):
                flat = turned[c].reshape(rows * SIDE, WIDTH).astype(jnp.bfloat16)
                if c != 1:
                    hidden_wide[plane, c, cells, :] = flat
                if rows == ROWS:
                    @pl.when(m == CHUNKS - 1)
                    def _():
                        hidden_wide[plane, c, 0:SIDE, :] = flat[SPAN - 2 * SIDE:SPAN - SIDE]
                        hidden_wide[plane, c, SIDE:2 * SIDE, :] = flat[SPAN - SIDE:]

    def give(j):
        return remote(
            result.at[:, theirs, part(j)], out.at[pl.ds(2 * rank, 2), :, part(j)],
            out_send.at[j], out_recv.at[j], sibling,
        )

    def keep(j):
        return pltpu.make_async_copy(
            result.at[:, own, part(j)], out.at[pl.ds(2 * rank, 2), :, part(j)], out_local.at[j]
        )

    def second(j):
        offsets = biases[0, 1:2, :] + biases[1, 1:2, :]
        total = product(hidden_wide, taps_two, j)
        for z in range(2):
            values = total[:, z * WIDTH:(z + 1) * WIDTH] + offsets
            values = values + field_wide[1 + z, 1, here(j), :].astype(jnp.float32)
            values = jnp.maximum(values, 0.0)
            result[z, :, part(j)] = values.T.astype(jnp.bfloat16)
        give(j).start()
        keep(j).start()

    receive(CHUNKS, head, 2)

    @pl.loop(1, CHUNKS + 1)
    def _(j):
        @pl.when(j < CHUNKS)
        def _():
            receive(j, lines(j), ROWS)

        @pl.when(j == CHUNKS)
        def _():
            receive(0, tail, ROWS - 2)

        second(lax.rem(j, CHUNKS))

    for up in (True, False):
        hand(CHUNKS, up, head).wait_send()
        hand(0, up, tail).wait_send()
        pl.loop(1, CHUNKS)(lambda m: hand(m, up, lines(m)).wait_send())

    @pl.loop(0, CHUNKS)
    def _(j):
        keep(j).wait()
        give(j).wait_send()
        pltpu.make_async_remote_copy(
            src_ref=result.at[:, theirs, part(j)],
            dst_ref=out.at[pl.ds(2 * other, 2), :, part(j)],
            send_sem=out_send.at[j], recv_sem=out_recv.at[j],
            device_id=sibling, device_id_type=MESH,
        ).wait_recv()


def body(field, conv_one, bias_one, conv_two, bias_two):
    rank = lax.axis_index("chan")
    pair = jnp.stack([bias_one, bias_two])
    own = (jnp.arange(2) == rank)[None, :, None]
    bias = jnp.where(own, pair[:, None, :], 0.0).reshape(2, WIDTH)
    bias = jnp.pad(bias, ((0, 6), (0, 0)))
    anywhere = pl.BlockSpec(memory_space=pl.ANY)
    bf16 = jnp.bfloat16
    padded = (SIDE + 2) * SIDE
    dma = pltpu.SemaphoreType.DMA
    return pl.pallas_call(
        functools.partial(kernel, lax.axis_size("slab")),
        out_shape=pltpu.VMEM(field.shape, field.dtype),
        in_specs=[anywhere] * 4,
        out_specs=pl.BlockSpec(memory_space=pltpu.VMEM),
        scratch_shapes=[
            pltpu.VMEM((4, WIDTH, CELLS), bf16),
            pltpu.VMEM((36 * WIDTH, 2 * WIDTH), bf16),
            pltpu.VMEM((36 * WIDTH, 2 * WIDTH), bf16),
            pltpu.VMEM((27, WIDTH, WIDTH), bf16),
            pltpu.VMEM((27, WIDTH, WIDTH), bf16),
            pltpu.VMEM((4, 3, padded, WIDTH), bf16),
            pltpu.VMEM((4, 3, padded, WIDTH), bf16),
            pltpu.VMEM((2, WIDTH, CELLS), bf16),
            pltpu.VMEM((2, 8, WIDTH), jnp.float32),
            dma((7,)),
            dma((3,)), dma((3,)), dma((3,)),
            dma((2, CHUNKS)), dma((2, CHUNKS)),
            dma((2, CHUNKS + 1)), dma((2, CHUNKS + 1)),
            dma((CHUNKS,)), dma((CHUNKS,)), dma((CHUNKS,)),
        ],
        compiler_params=pltpu.CompilerParams(
            collective_id=0, has_side_effects=True, vmem_limit_bytes=56 * 2**20
        ),
        cost_estimate=pl.CostEstimate(
            flops=2 * 2 * 2 * CELLS * WIDTH * 27 * WIDTH, bytes_accessed=8 * 2**20,
            transcendentals=0,
        ),
    )(field, conv_one.reshape(27, HALF, WIDTH), conv_two.reshape(27, WIDTH, WIDTH), bias)


def solution(mesh):
    return jax.shard_map(
        body,
        mesh=mesh,
        in_specs=(
            P(("box", "slab"), "chan", None),
            P(None, None, None, "chan", None),
            P("chan"),
            P(),
            P("chan"),
        ),
        out_specs=P(("box", "slab"), "chan", None),
        check_vma=False,
    )
```
